32 devices in a mesh: groups: 2 (over x), mom: 16 (over z, y, core).
Axes of the slice: x: 2, y: 2, z: 4, core: 2. Of those that a mesh axis runs over, the one named last changes fastest.
Arguments:
- sink_fields: bfloat16 [192, 2, 384, 384], P('groups', None, 'mom'), parts along dimension 0
- source_fields: bfloat16 [192, 2, 384, 384], P('groups', None, 'mom'), parts along dimension 0
- momenta: int32 [6, 24], replicated, may hold values from 0 to 95
- pair_list: int32 [16, 8, 2], replicated, may hold values from 0 to 23
- live_pairs: int32 [16], replicated, may hold values from 1 to 8, as said below
Outputs:
- correlators: float32 [32, 2, 8, 8], P(('groups', 'mom')), parts along dimension 0
The draws below stay inside these ranges and needn't reach their ends.
There are 2 independent parts, one for each index of `groups`. The reference program is written for one: setup_inputs(seed, part) draws one part's arguments, and reference() takes and returns one part's arrays. A program takes and returns all parts, laid end to end along the dimension named above; an argument that names none is the same for every part. Nothing has to cross between parts.
Inputs may be any that keep to these rules, and one draw needn't show every extreme that they name: live_pairs[s] counts the used slots of sector s; slots from it on are ignored. In every draw at least one sector has all 8 slots used. `momenta`: sector s belongs to frame s mod 6. `pair_list`: labels index the sector's frame list.
All inputs are finite; a program needn't handle non-finite values.
Results may differ from the reference program's by a relative error of at most 0.0042.
Values may be sent and summed in bfloat16 or wider, within the bound.
A program may use at most 128 MiB of HBM per device.

```python
import math
import jax
import jax.numpy as jnp
from jax import lax

NV = 384
NMOM = 96
FRAMES = 6
LABELS = 24
PAIRS = 8
SEC_DEV = 1
NSEC = 16


def field_values(key, noise, spread):
    row_key, column_key = jax.random.split(key)
    positions = jnp.arange(NV, dtype=jnp.float32)
    rising = jnp.exp(math.log(3.0) * positions / (NV - 1))
    row_scale = rising[None, None, :, None] * jnp.exp(jax.random.uniform(row_key, (NMOM, 1, NV, 1), jnp.float32) * math.log(spread))
    column_scale = jnp.exp(jax.random.uniform(column_key, (NMOM, 1, 1, NV), jnp.float32) * math.log(spread))
    return noise * row_scale * column_scale / math.sqrt(2.0 * NV)


def field_draw(key):
    noise_key, scale_key = jax.random.split(key)
    field_shape = (NMOM, 2, NV, NV)
    noise = jnp.clip(jax.random.normal(noise_key, field_shape, jnp.float32), -6.0, 6.0)
    return field_values(scale_key, noise, 10.0)


def draw_sink_fields(key, part):
    key = jax.random.fold_in(key, 11)
    return field_draw(key).astype(jnp.bfloat16)


def draw_source_fields(key, part):
    key = jax.random.fold_in(key, 13)
    return field_draw(key).astype(jnp.bfloat16)


def draw_live_pairs(key, part):
    key = jax.random.fold_in(key, 5)
    full_key, small_key, block_key = jax.random.split(key, 3)
    full_slot = jax.random.randint(full_key, (NSEC,), 0, 3) == 0
    small_count = jax.random.randint(small_key, (NSEC,), 1, 3)
    counted = jnp.where(full_slot, PAIRS, small_count)
    chosen = jax.random.randint(block_key, (), 0, NSEC // SEC_DEV)
    owner_block = jnp.arange(NSEC, dtype=jnp.int32) // SEC_DEV
    return jnp.where(owner_block == chosen, PAIRS, counted).astype(jnp.int32)


def plant(array, stream_key, smallest, largest):
    place = [jax.random.randint(jax.random.fold_in(stream_key, axis), (), 0, length) for axis, length in enumerate(array.shape)]
    widest = array.shape.index(max(array.shape))
    neighbour = place[:widest] + [(place[widest] + 1) % array.shape[widest]] + place[widest + 1:]
    return array.at[tuple(place)].set(smallest).at[tuple(neighbour)].set(largest)


def setup_inputs(seed: int = 0, part: int = 0) -> dict:
    key_list = jax.random.split(jax.random.key(seed), 6)
    part_keys = jax.random.split(jax.random.fold_in(key_list[5], part), 6)
    return {
        "sink_fields": draw_sink_fields(jax.random.fold_in(jax.random.fold_in(key_list[5], part), 71), part),
        "source_fields": draw_source_fields(jax.random.fold_in(jax.random.fold_in(key_list[5], part), 71), part),
        "momenta": plant(jax.random.randint(key_list[2], (FRAMES, LABELS), 0, NMOM), jax.random.fold_in(key_list[2], 1), 0, NMOM - 1).astype(jnp.int32),
        "pair_list": plant(jax.random.randint(key_list[3], (NSEC, PAIRS, 2), 0, LABELS), jax.random.fold_in(key_list[3], 1), 0, LABELS - 1).astype(jnp.int32),
        "live_pairs": draw_live_pairs(jax.random.fold_in(key_list[5], 71), part),
    }


def field_weights(fields):
    squares = lax.optimization_barrier(jnp.sum(jnp.square(fields.astype(jnp.float32)), axis=(1, 2, 3)))
    return 1.0 / jnp.sqrt(squares / NV + 1e-06)

def reference(sink_fields, source_fields, momenta, pair_list, live_pairs):
    weight_a = field_weights(sink_fields)
    weight_b = field_weights(source_fields)
    sectors = jnp.arange(NSEC, dtype=jnp.int32)
    listed = jnp.take(momenta, sectors % FRAMES, axis=0)
    first_field = jnp.take_along_axis(listed, pair_list[:, :, 0], axis=1).astype(jnp.int32)
    second_field = jnp.take_along_axis(listed, pair_list[:, :, 1], axis=1).astype(jnp.int32)
    live_slot = jnp.arange(PAIRS, dtype=jnp.int32)[None, :] < live_pairs[:, None]

    def multiply(indices):
        block_a = sink_fields[indices[0]]
        block_b = source_fields[indices[1]]
        real_part = jnp.dot(block_a[0], block_b[0], preferred_element_type=jnp.float32) - jnp.dot(block_a[1], block_b[1], preferred_element_type=jnp.float32)
        imag_part = jnp.dot(block_a[0], block_b[1], preferred_element_type=jnp.float32) + jnp.dot(block_a[1], block_b[0], preferred_element_type=jnp.float32)
        joined = jnp.stack([real_part, imag_part]) * weight_a[indices[0]] * weight_b[indices[1]]
        return joined.astype(jnp.bfloat16)

    def blank_slot(indices):
        return jnp.zeros((2, NV, NV), jnp.bfloat16)

    def slot_product(item):
        index_a, index_b, alive = item
        return lax.cond(alive, multiply, blank_slot, (index_a, index_b))

    def contract(left_rows, right_rows):
        return jnp.einsum('prc,qrc->pq', left_rows, right_rows, precision=lax.Precision.HIGHEST)

    def sector_gram(item):
        products = lax.map(slot_product, item).astype(jnp.float32)
        turned = jnp.swapaxes(products, 2, 3)
        real_part = contract(products[:, 0], turned[:, 0]) - contract(products[:, 1], turned[:, 1])
        imag_part = contract(products[:, 0], turned[:, 1]) + contract(products[:, 1], turned[:, 0])
        return jnp.stack([real_part, imag_part])
    return lax.map(sector_gram, (first_field, second_field, live_slot))
```

```python
import functools

import jax
import jax.numpy as jnp
from jax import lax
from jax.experimental import pallas as pl
from jax.experimental.pallas import tpu as pltpu
from jax.sharding import PartitionSpec as P


def complex_block(field_pair):
    eigen_width = field_pair.shape[-1]
    left_block = jnp.concatenate([field_pair[0, 0], field_pair[0, 1]], axis=1)
    upper_half = jnp.concatenate([field_pair[1, 0], field_pair[1, 1]], axis=1)
    lower_half = jnp.concatenate([-field_pair[1, 1], field_pair[1, 0]], axis=1)
    right_block = jnp.concatenate([upper_half, lower_half], axis=0)
    joined = jnp.dot(left_block, right_block, preferred_element_type=jnp.float32)
    return jnp.stack([joined[:, :eigen_width], joined[:, eigen_width:]])


def slot_products(blocks):
    item_count = blocks.shape[1]
    eigen_width = blocks.shape[-1]
    storage = jnp.zeros((item_count, 2, eigen_width, eigen_width), jnp.float32)
    slot_blocks = blocks[0]

    def blank_slot(field_pair):
        return jnp.zeros((2, eigen_width, eigen_width), jnp.float32)

    def one_slot(item_index, held_items):
        field_pair = lax.dynamic_index_in_dim(slot_blocks, item_index, 0, keepdims=False)
        result = lax.cond(jnp.any(field_pair != 0), complex_block, blank_slot, field_pair)
        return lax.dynamic_update_index_in_dim(held_items, result, item_index, 0)

    return lax.fori_loop(0, item_count, one_slot, storage)


def contract(left_rows, right_rows):
    return jnp.einsum("spx,sqx->spq", left_rows, right_rows, preferred_element_type=jnp.float32)


def dense_plan(sink_fields, source_fields, momenta, pair_list, live_pairs):
    devices = lax.axis_size("mom")
    position = lax.axis_index("mom")
    sector_count = live_pairs.shape[0]
    owned_count = sector_count // devices
    pair_slots = pair_list.shape[1]
    frames = momenta.shape[0]
    rows_here = sink_fields.shape[2]
    eigen_width = sink_fields.shape[3]
    squares_sink = jnp.sum(jnp.square(sink_fields.astype(jnp.float32)), axis=(1, 2, 3))
    squares_source = jnp.sum(jnp.square(source_fields.astype(jnp.float32)), axis=(1, 2, 3))
    norm_a, norm_b = lax.psum((squares_sink, squares_source), "mom")
    weight_a = 1.0 / jnp.sqrt(norm_a / eigen_width + 1e-06)
    weight_b = 1.0 / jnp.sqrt(norm_b / eigen_width + 1e-06)
    sectors = jnp.arange(sector_count, dtype=jnp.int32)
    labels = jnp.take(pair_list, sectors, axis=0)
    listed = jnp.take(momenta, sectors % frames, axis=0)
    first_field = jnp.take_along_axis(listed, labels[:, :, 0], axis=1)
    second_field = jnp.take_along_axis(listed, labels[:, :, 1], axis=1)
    live_slot = (
        jnp.arange(pair_slots, dtype=jnp.int32)[None, :] < jnp.take(live_pairs, sectors)[:, None]
    )
    live_mask = live_slot.reshape(-1)[:, None, None, None]
    part_sink = jnp.where(live_mask, jnp.take(sink_fields, first_field.reshape(-1), axis=0), 0)
    part_source = jnp.where(live_mask, jnp.take(source_fields, second_field.reshape(-1), axis=0), 0)
    packed = jnp.stack([part_sink, part_source], axis=1).reshape(
        devices, owned_count * pair_slots, 2, 2, rows_here, eigen_width
    )
    products = slot_products(lax.all_to_all(packed, "mom", split_axis=0, concat_axis=4, tiled=True))
    mine_first = lax.dynamic_slice_in_dim(
        first_field, position * owned_count, owned_count, 0
    ).reshape(-1)
    mine_second = lax.dynamic_slice_in_dim(
        second_field, position * owned_count, owned_count, 0
    ).reshape(-1)
    scale_sink = jnp.take(weight_a, mine_first)
    scale_source = jnp.take(weight_b, mine_second)
    shaped = (
        products * scale_sink[:, None, None, None] * scale_source[:, None, None, None]
    ).astype(jnp.bfloat16)
    flattened = shaped.reshape(owned_count, pair_slots, 2, eigen_width * eigen_width)
    turned = jnp.swapaxes(shaped, 2, 3).reshape(
        owned_count, pair_slots, 2, eigen_width * eigen_width
    )
    real_part = contract(flattened[:, :, 0], turned[:, :, 0]) - contract(
        flattened[:, :, 1], turned[:, :, 1]
    )
    imag_part = contract(flattened[:, :, 0], turned[:, :, 1]) + contract(
        flattened[:, :, 1], turned[:, :, 0]
    )
    gram_blocks = jnp.stack([real_part, imag_part], axis=1)
    return gram_blocks


LIGHT = 2
HEAVY_PLANS = (4, 6, 8, 16)
CHUNK = 16


def rank_of_device(device):
    upper, lower, side, core = device // 8, (device // 4) % 2, (device // 2) % 2, device % 2
    return core * 8 + ((upper + lower + 1) % 2) * 4 + ((side + upper) % 2) * 2 + upper


def device_of_rank(rank):
    core, outer, turn, upper = rank // 8, (rank // 4) % 2, (rank // 2) % 2, rank % 2
    return upper * 8 + ((outer + upper + 1) % 2) * 4 + ((turn + upper) % 2) * 2 + core


def sector_kernel(
    heavy, rows, order, ranks, momenta, pairs, live, sink_hbm, source_hbm, out_ref,
    sink, source, packed, recv, product, turned_re, turned_im, grams,
    load_sem, send_sem, recv_sem, gram_send, gram_recv,
):
    devices, slots, width = grams.shape[0], product.shape[0], sink.shape[2]
    frames = momenta.shape[0]
    field_rows = 2 * rows
    me = lax.axis_index("mom")
    my_rank = rank_of_device(me)
    is_heavy = (my_rank < heavy).astype(jnp.int32)

    loads = [
        pltpu.make_async_copy(sink_hbm, sink, load_sem.at[0]),
        pltpu.make_async_copy(source_hbm, source, load_sem.at[1]),
    ]
    for load in loads:
        load.start()
    barrier = pltpu.get_barrier_semaphore()

    @pl.loop(1, devices)
    def _(step):
        pl.semaphore_signal(barrier, inc=1, device_id={"mom": (me + step) % devices})

    pl.semaphore_wait(barrier, devices - 1)
    for load in loads:
        load.wait()

    def fill(target, device, slot):
        sector = order[rank_of_device(device)]
        frame = sector % frames
        target[pl.ds(0, field_rows), :] = sink[momenta[frame, pairs[sector, 2 * slot]]]
        target[pl.ds(field_rows, field_rows), :] = source[momenta[frame, pairs[sector, 2 * slot + 1]]]

    def send(device, slot):
        fill(packed.at[slot, device], device, slot)
        pltpu.make_async_remote_copy(
            src_ref=packed.at[slot, device],
            dst_ref=recv.at[slot, me],
            send_sem=send_sem.at[slot],
            recv_sem=recv_sem.at[slot],
            device_id={"mom": device},
        ).start()

    @pl.loop(0, LIGHT)
    def _(slot):
        fill(recv.at[slot, me], me, slot)

        @pl.loop(1, devices)
        def _(step):
            send((me + step) % devices, slot)

    @pl.loop(LIGHT, slots)
    def _(slot):
        @pl.loop(0, heavy)
        def _(step):
            device = device_of_rank((my_rank + step) % heavy)

            @pl.when(device != me)
            def _():
                send(device, slot)

            @pl.when(device == me)
            def _():
                fill(recv.at[slot, me], me, slot)

    product[pl.ds(LIGHT, slots - LIGHT)] = jnp.zeros((slots - LIGHT, width, 2 * width), product.dtype)
    turned_re[pl.ds(LIGHT, slots - LIGHT)] = jnp.zeros((slots - LIGHT, width, 2 * width), product.dtype)
    turned_im[pl.ds(LIGHT, slots - LIGHT)] = jnp.zeros((slots - LIGHT, width, 2 * width), product.dtype)

    used = live[order[my_rank]]

    def parts(slot, start):
        field = recv[slot, :, pl.ds(start, field_rows), :].astype(jnp.float32)
        norm = jnp.sum(jnp.sum(jnp.square(field), axis=(0, 1), keepdims=True)[0], axis=1, keepdims=True)
        weight = 1.0 / jnp.sqrt(norm / width + 1e-06)
        field = field.reshape(devices, 2, rows, width)
        real = field[:, 0].reshape(width, width).astype(jnp.bfloat16)
        imag = field[:, 1].reshape(width, width).astype(jnp.bfloat16)
        return real, imag, weight

    def work(slot, carry):
        arrived = recv.at[slot, pl.ds(0, devices - 1)]
        pltpu.make_async_copy(arrived, arrived, recv_sem.at[slot]).wait()
        a_re, a_im, weight_a = parts(slot, 0)
        b_re, b_im, weight_b = parts(slot, field_rows)
        left = jnp.concatenate([a_re, a_im], axis=1)
        right = jnp.concatenate(
            [jnp.concatenate([b_re, b_im], axis=1), jnp.concatenate([-b_im, b_re], axis=1)], axis=0
        )
        joined = jnp.dot(left, right, preferred_element_type=jnp.float32)
        joined = joined * weight_a * weight_b
        joined = jnp.where(slot < used, joined, 0.0)
        product[slot] = joined.astype(jnp.bfloat16)
        real = joined[:, :width].T.astype(jnp.bfloat16)
        imag = joined[:, width:].T.astype(jnp.bfloat16)
        turned_re[slot] = jnp.concatenate([real, -imag], axis=1)
        turned_im[slot] = jnp.concatenate([imag, real], axis=1)
        return carry

    lax.fori_loop(0, LIGHT + (slots - LIGHT) * is_heavy, work, 0)

    side = slots * CHUNK
    along = (((1,), (1,)), ((), ()))

    def gather_chunk(index, sums):
        start = pl.ds(pl.multiple_of(index * CHUNK, CHUNK), CHUNK)
        left = product[:, start, :].reshape(side, 2 * width)
        right_re = turned_re[:, start, :].reshape(side, 2 * width)
        right_im = turned_im[:, start, :].reshape(side, 2 * width)
        return (
            sums[0] + lax.dot_general(left, right_re, along, preferred_element_type=jnp.float32),
            sums[1] + lax.dot_general(left, right_im, along, preferred_element_type=jnp.float32),
        )

    blank = jnp.zeros((side, side), jnp.float32)
    sums = lax.fori_loop(0, width // CHUNK, gather_chunk, (blank, blank))
    row = lax.broadcasted_iota(jnp.int32, (side, side), 0) % CHUNK
    column = lax.broadcasted_iota(jnp.int32, (side, side), 1) % CHUNK
    for part in range(2):
        kept = jnp.where(row == column, sums[part], 0.0)
        grams[me, part] = jnp.sum(kept.reshape(slots, CHUNK, side), axis=1)

    @pl.loop(1, devices)
    def _(step):
        pltpu.make_async_remote_copy(
            src_ref=grams.at[me],
            dst_ref=grams.at[me],
            send_sem=gram_send,
            recv_sem=gram_recv,
            device_id={"mom": (me + step) % devices},
        ).start()

    for semaphore in (gram_send, gram_recv):
        moved = grams.at[pl.ds(0, devices - 1)]
        pltpu.make_async_copy(moved, moved, semaphore).wait()

    @pl.loop(0, LIGHT)
    def _(slot):
        gone = packed.at[slot, pl.ds(0, devices - 1)]
        pltpu.make_async_copy(gone, gone, send_sem.at[slot]).wait()

    @pl.loop(LIGHT, slots)
    def _(slot):
        @pl.loop(0, heavy - is_heavy)
        def _(step):
            gone = packed.at[slot, 0]
            pltpu.make_async_copy(gone, gone, send_sem.at[slot]).wait()

    out_ref[...] = grams[device_of_rank(ranks[me])]


def sector_call(number, heavy, rows, devices, slots, width, operands):
    fields = operands[-1].shape[0]
    piece = 4 * rows
    smem = pl.BlockSpec(memory_space=pltpu.SMEM)
    hbm = pl.BlockSpec(memory_space=pl.ANY)
    low = jnp.bfloat16
    return pl.pallas_call(
        functools.partial(sector_kernel, heavy, rows),
        out_shape=jax.ShapeDtypeStruct((2, slots, slots * CHUNK), jnp.float32),
        in_specs=[smem] * 5 + [hbm] * 2,
        out_specs=pl.BlockSpec(memory_space=pltpu.VMEM),
        scratch_shapes=[
            pltpu.VMEM((fields, 2 * rows, width), low),
            pltpu.VMEM((fields, 2 * rows, width), low),
            pltpu.VMEM((slots, devices, piece, width), low),
            pltpu.VMEM((slots, devices, piece, width), low),
            pltpu.VMEM((slots, width, 2 * width), low),
            pltpu.VMEM((slots, width, 2 * width), low),
            pltpu.VMEM((slots, width, 2 * width), low),
            pltpu.VMEM((devices, 2, slots, slots * CHUNK), jnp.float32),
            pltpu.SemaphoreType.DMA((2,)),
            pltpu.SemaphoreType.DMA((slots,)),
            pltpu.SemaphoreType.DMA((slots,)),
            pltpu.SemaphoreType.DMA,
            pltpu.SemaphoreType.DMA,
        ],
        compiler_params=pltpu.CompilerParams(
            collective_id=number, has_side_effects=True, vmem_limit_bytes=58 * 2**20
        ),
        cost_estimate=pl.CostEstimate(
            flops=slots * 8 * width**3, bytes_accessed=4 * fields * rows * width * 2, transcendentals=0
        ),
    )(*operands)


def ranked_plan(sink_fields, source_fields, momenta, pair_list, live_pairs):
    devices = lax.axis_size("mom")
    fields, _, rows, width = sink_fields.shape
    slots = pair_list.shape[1]
    places = jnp.arange(devices, dtype=jnp.int32)
    ahead = (live_pairs[None, :] > live_pairs[:, None]) | (
        (live_pairs[None, :] == live_pairs[:, None]) & (places[None, :] < places[:, None])
    )
    ranks = jnp.sum(ahead.astype(jnp.int32), axis=1)
    order = jnp.sum(jnp.where(ranks[None, :] == places[:, None], places[None, :], 0), axis=1)
    crowded = jnp.sum((live_pairs > LIGHT).astype(jnp.int32))
    choice = sum((crowded > plan).astype(jnp.int32) for plan in HEAVY_PLANS[:-1])
    operands = (
        order, ranks, momenta, pair_list.reshape(devices, 2 * slots), live_pairs,
        sink_fields.reshape(fields, 2 * rows, width), source_fields.reshape(fields, 2 * rows, width),
    )
    branches = [
        functools.partial(
            lambda number, heavy, *given: sector_call(number, heavy, rows, devices, slots, width, given),
            number, heavy,
        )
        for number, heavy in enumerate(HEAVY_PLANS)
    ]
    grams = lax.switch(choice, branches, *operands)
    return jnp.sum(grams.reshape(1, 2, slots, slots, CHUNK), axis=-1)


def on_device(sink_fields, source_fields, momenta, pair_list, live_pairs):
    fits = (
        lax.axis_size("mom") == 16
        and pair_list.shape[0] == 16
        and pair_list.shape[1] == 8
        and sink_fields.shape[2] % 8 == 0
        and sink_fields.shape[3] % 128 == 0
    )
    plan = ranked_plan if fits else dense_plan
    return plan(sink_fields, source_fields, momenta, pair_list, live_pairs)


def solution(mesh):
    return jax.shard_map(
        on_device,
        mesh=mesh,
        in_specs=(P("groups", None, "mom", None), P("groups", None, "mom", None), P(), P(), P()),
        out_specs=P(("groups", "mom"), None, None, None),
        check_vma=False,
    )
```

```python
import functools

import jax
import jax.numpy as jnp
from jax import lax
from jax.experimental import pallas as pl
from jax.experimental.pallas import tpu as pltpu
from jax.sharding import PartitionSpec as P


def complex_block(field_pair):
    eigen_width = field_pair.shape[-1]
    left_block = jnp.concatenate([field_pair[0, 0], field_pair[0, 1]], axis=1)
    upper_half = jnp.concatenate([field_pair[1, 0], field_pair[1, 1]], axis=1)
    lower_half = jnp.concatenate([-field_pair[1, 1], field_pair[1, 0]], axis=1)
    right_block = jnp.concatenate([upper_half, lower_half], axis=0)
    joined = jnp.dot(left_block, right_block, preferred_element_type=jnp.float32)
    return jnp.stack([joined[:, :eigen_width], joined[:, eigen_width:]])


def slot_products(blocks):
    item_count = blocks.shape[1]
    eigen_width = blocks.shape[-1]
    storage = jnp.zeros((item_count, 2, eigen_width, eigen_width), jnp.float32)
    slot_blocks = blocks[0]

    def blank_slot(field_pair):
        return jnp.zeros((2, eigen_width, eigen_width), jnp.float32)

    def one_slot(item_index, held_items):
        field_pair = lax.dynamic_index_in_dim(slot_blocks, item_index, 0, keepdims=False)
        result = lax.cond(jnp.any(field_pair != 0), complex_block, blank_slot, field_pair)
        return lax.dynamic_update_index_in_dim(held_items, result, item_index, 0)

    return lax.fori_loop(0, item_count, one_slot, storage)


def contract(left_rows, right_rows):
    return jnp.einsum("spx,sqx->spq", left_rows, right_rows, preferred_element_type=jnp.float32)


def dense_plan(sink_fields, source_fields, momenta, pair_list, live_pairs):
    devices = lax.axis_size("mom")
    position = lax.axis_index("mom")
    sector_count = live_pairs.shape[0]
    owned_count = sector_count // devices
    pair_slots = pair_list.shape[1]
    frames = momenta.shape[0]
    rows_here = sink_fields.shape[2]
    eigen_width = sink_fields.shape[3]
    squares_sink = jnp.sum(jnp.square(sink_fields.astype(jnp.float32)), axis=(1, 2, 3))
    squares_source = jnp.sum(jnp.square(source_fields.astype(jnp.float32)), axis=(1, 2, 3))
    norm_a, norm_b = lax.psum((squares_sink, squares_source), "mom")
    weight_a = 1.0 / jnp.sqrt(norm_a / eigen_width + 1e-06)
    weight_b = 1.0 / jnp.sqrt(norm_b / eigen_width + 1e-06)
    sectors = jnp.arange(sector_count, dtype=jnp.int32)
    labels = jnp.take(pair_list, sectors, axis=0)
    listed = jnp.take(momenta, sectors % frames, axis=0)
    first_field = jnp.take_along_axis(listed, labels[:, :, 0], axis=1)
    second_field = jnp.take_along_axis(listed, labels[:, :, 1], axis=1)
    live_slot = (
        jnp.arange(pair_slots, dtype=jnp.int32)[None, :] < jnp.take(live_pairs, sectors)[:, None]
    )
    live_mask = live_slot.reshape(-1)[:, None, None, None]
    part_sink = jnp.where(live_mask, jnp.take(sink_fields, first_field.reshape(-1), axis=0), 0)
    part_source = jnp.where(live_mask, jnp.take(source_fields, second_field.reshape(-1), axis=0), 0)
    packed = jnp.stack([part_sink, part_source], axis=1).reshape(
        devices, owned_count * pair_slots, 2, 2, rows_here, eigen_width
    )
    products = slot_products(lax.all_to_all(packed, "mom", split_axis=0, concat_axis=4, tiled=True))
    mine_first = lax.dynamic_slice_in_dim(
        first_field, position * owned_count, owned_count, 0
    ).reshape(-1)
    mine_second = lax.dynamic_slice_in_dim(
        second_field, position * owned_count, owned_count, 0
    ).reshape(-1)
    scale_sink = jnp.take(weight_a, mine_first)
    scale_source = jnp.take(weight_b, mine_second)
    shaped = (
        products * scale_sink[:, None, None, None] * scale_source[:, None, None, None]
    ).astype(jnp.bfloat16)
    flattened = shaped.reshape(owned_count, pair_slots, 2, eigen_width * eigen_width)
    turned = jnp.swapaxes(shaped, 2, 3).reshape(
        owned_count, pair_slots, 2, eigen_width * eigen_width
    )
    real_part = contract(flattened[:, :, 0], turned[:, :, 0]) - contract(
        flattened[:, :, 1], turned[:, :, 1]
    )
    imag_part = contract(flattened[:, :, 0], turned[:, :, 1]) + contract(
        flattened[:, :, 1], turned[:, :, 0]
    )
    gram_blocks = jnp.stack([real_part, imag_part], axis=1)
    return gram_blocks


PLANS = ((4, 8), (5, 8), (6, 8), (7, 7), (8, 8), (10, 6), (16, 0))
CHUNK = 64


def place_of_device(device):
    upper, lower, side, core = device // 8, (device // 4) % 2, (device // 2) % 2, device % 2
    return core * 8 + ((upper + lower + 1) % 2) * 4 + ((side + upper) % 2) * 2 + upper


def device_of_place(place):
    core, outer, turn, upper = place // 8, (place // 4) % 2, (place // 2) % 2, place % 2
    return upper * 8 + ((outer + upper + 1) % 2) * 4 + ((turn + upper) % 2) * 2 + core


def rank_of_place(heavy, devices, place):
    if heavy % 2 == 0:
        return place
    light = place - heavy
    moved = heavy + light // 2 + (light % 2) * ((devices + 1 - heavy) // 2)
    return jnp.where(light < 0, place, moved)


def place_of_rank(heavy, devices, rank):
    if heavy % 2 == 0:
        return rank
    light, first = rank - heavy, (devices + 1 - heavy) // 2
    moved = jnp.where(light < first, heavy + 2 * light, heavy + 1 + 2 * (light - first))
    return jnp.where(light < 0, rank, moved)


def sector_kernel(
    heavy, double, rows, order, ranks, momenta, pairs, live, sink_hbm, source_hbm, out_ref,
    sink, source, packed, recv, product, turned, grams,
    load_sem, send_sem, recv_sem, gram_send, gram_recv,
):
    devices, slots, width = grams.shape[0], product.shape[0], sink.shape[2]
    frames = momenta.shape[0]
    field_rows = 2 * rows
    me = lax.axis_index("mom")
    half = devices // 2
    my_half = me // half

    def rank_of_device(device):
        return rank_of_place(heavy, devices, place_of_device(device))

    my_rank = rank_of_device(me)
    is_heavy = (my_rank < heavy).astype(jnp.int32)
    is_double = (my_rank < heavy + double).astype(jnp.int32)

    loads = [
        pltpu.make_async_copy(sink_hbm, sink, load_sem.at[0]),
        pltpu.make_async_copy(source_hbm, source, load_sem.at[1]),
    ]
    for load in loads:
        load.start()
    barrier = pltpu.get_barrier_semaphore()

    @pl.loop(1, devices)
    def _(step):
        pl.semaphore_signal(barrier, inc=1, device_id={"mom": (me + step) % devices})

    pl.semaphore_wait(barrier, devices - 1)
    for load in loads:
        load.wait()

    def fill(target, device, slot):
        sector = order[rank_of_device(device)]
        frame = sector % frames
        target[pl.ds(0, field_rows), :] = sink[momenta[frame, pairs[sector, slot, 0]]]
        target[pl.ds(field_rows, field_rows), :] = source[momenta[frame, pairs[sector, slot, 1]]]

    def send(device, slot):
        fill(packed.at[slot, device], device, slot)
        pltpu.make_async_remote_copy(
            src_ref=packed.at[slot, device],
            dst_ref=recv.at[slot, me],
            send_sem=send_sem.at[slot],
            recv_sem=recv_sem.at[slot],
            device_id={"mom": device},
        ).start()

    for slot in range(2):
        fill(recv.at[slot, me], me, slot)

        @pl.loop(0, devices)
        def _(step):
            device = ((my_half + 1 + step // half) % 2) * half + (me + step) % half
            sends = device != me
            if slot == 1:
                sends = sends & (rank_of_device(device) < heavy + double)

            @pl.when(sends)
            def _():
                send(device, slot)

    @pl.loop(2, slots)
    def _(slot):
        for near in range(2):
            parity = (my_half + 1 + near) % 2
            count = (heavy + 1 - parity) // 2

            @pl.loop(0, count)
            def _(step):
                device = device_of_place(2 * ((me + step) % count) + parity)

                @pl.when(device != me)
                def _():
                    send(device, slot)

                @pl.when(device == me)
                def _():
                    fill(recv.at[slot, me], me, slot)

    product[pl.ds(1, slots - 1)] = jnp.zeros((slots - 1, width, 2 * width), product.dtype)

    used = live[order[my_rank]]

    def parts(slot, start):
        field = recv[slot, :, pl.ds(start, field_rows), :].astype(jnp.float32)
        norm = jnp.sum(jnp.sum(jnp.square(field), axis=(0, 1), keepdims=True)[0], axis=1, keepdims=True)
        weight = 1.0 / jnp.sqrt(norm / width + 1e-06)
        field = field.reshape(devices, 2, rows, width)
        real = field[:, 0].reshape(width, width).astype(jnp.bfloat16)
        imag = field[:, 1].reshape(width, width).astype(jnp.bfloat16)
        return real, imag, weight

    def work(slot, gram):
        arrived = recv.at[slot, pl.ds(0, devices - 1)]
        pltpu.make_async_copy(arrived, arrived, recv_sem.at[slot]).wait()
        a_re, a_im, weight_a = parts(slot, 0)
        b_re, b_im, weight_b = parts(slot, field_rows)
        left = jnp.concatenate([a_re, a_im], axis=1)
        right = jnp.concatenate(
            [jnp.concatenate([b_re, b_im], axis=1), jnp.concatenate([-b_im, b_re], axis=1)], axis=0
        )
        joined = jnp.dot(left, right, preferred_element_type=jnp.float32)
        joined = joined * weight_a * weight_b
        joined = jnp.where(slot < used, joined, 0.0)
        product[slot] = joined.astype(jnp.bfloat16)
        real = joined[:, :width].T.astype(jnp.bfloat16)
        imag = joined[:, width:].T.astype(jnp.bfloat16)
        turned[0] = jnp.concatenate([real, -imag], axis=1)
        turned[1] = jnp.concatenate([imag, real], axis=1)
        sums = jnp.zeros((slots * CHUNK, 2 * CHUNK), jnp.float32)
        for start in range(0, width, CHUNK):
            left_rows = product[:, start : start + CHUNK, :].reshape(slots * CHUNK, 2 * width)
            right_rows = turned[:, start : start + CHUNK, :].reshape(2 * CHUNK, 2 * width)
            sums += lax.dot_general(
                left_rows, right_rows, (((1,), (1,)), ((), ())), preferred_element_type=jnp.float32
            )
        row = lax.broadcasted_iota(jnp.int32, sums.shape, 0) % CHUNK
        column = lax.broadcasted_iota(jnp.int32, sums.shape, 1)
        kept = jnp.where(row == column % CHUNK, sums, 0.0).reshape(slots, CHUNK, 2 * CHUNK)
        kept = jnp.sum(kept, axis=1)
        first_part = lax.broadcasted_iota(jnp.int32, kept.shape, 1) < CHUNK
        real_sum = jnp.sum(jnp.where(first_part, kept, 0.0), axis=1, keepdims=True)
        imag_sum = jnp.sum(jnp.where(first_part, 0.0, kept), axis=1, keepdims=True)
        place = place_in_row - slot
        gram = gram + jnp.where(place == 0, real_sum, 0.0) + jnp.where(place == slots, imag_sum, 0.0)
        return gram

    tile = (slots, 2 * slots * slots)
    place_in_row = lax.broadcasted_iota(jnp.int32, tile, 1) - 2 * slots * lax.broadcasted_iota(jnp.int32, tile, 0)
    gram = lax.fori_loop(0, 1 + is_double + (slots - 2) * is_heavy, work, jnp.zeros(tile, jnp.float32))
    grams[me] = jnp.sum(gram, axis=0, keepdims=True)

    @pl.loop(1, devices)
    def _(step):
        pltpu.make_async_remote_copy(
            src_ref=grams.at[me],
            dst_ref=grams.at[me],
            send_sem=gram_send,
            recv_sem=gram_recv,
            device_id={"mom": (me + step) % devices},
        ).start()

    for semaphore in (gram_send, gram_recv):
        moved = grams.at[pl.ds(0, devices - 1)]
        pltpu.make_async_copy(moved, moved, semaphore).wait()

    for slot in range(slots):
        sent = devices - 1 if slot == 0 else heavy + double - is_double if slot == 1 else heavy - is_heavy

        @pl.loop(0, sent)
        def _(step):
            gone = packed.at[slot, 0]
            pltpu.make_async_copy(gone, gone, send_sem.at[slot]).wait()

    out_ref[...] = grams[device_of_place(place_of_rank(heavy, devices, ranks[me]))]


def sector_call(number, heavy, double, rows, devices, slots, width, operands):
    fields = operands[-1].shape[0]
    piece = 4 * rows
    smem = pl.BlockSpec(memory_space=pltpu.SMEM)
    hbm = pl.BlockSpec(memory_space=pl.ANY)
    low = jnp.bfloat16
    return pl.pallas_call(
        functools.partial(sector_kernel, heavy, double, rows),
        out_shape=jax.ShapeDtypeStruct((1, 2 * slots * slots), jnp.float32),
        in_specs=[smem] * 5 + [hbm] * 2,
        out_specs=pl.BlockSpec(memory_space=pltpu.VMEM),
        scratch_shapes=[
            pltpu.VMEM((fields, 2 * rows, width), low),
            pltpu.VMEM((fields, 2 * rows, width), low),
            pltpu.VMEM((slots, devices, piece, width), low),
            pltpu.VMEM((slots, devices, piece, width), low),
            pltpu.VMEM((slots, width, 2 * width), low),
            pltpu.VMEM((2, width, 2 * width), low),
            pltpu.VMEM((devices, 1, 2 * slots * slots), jnp.float32),
            pltpu.SemaphoreType.DMA((2,)),
            pltpu.SemaphoreType.DMA((slots,)),
            pltpu.SemaphoreType.DMA((slots,)),
            pltpu.SemaphoreType.DMA,
            pltpu.SemaphoreType.DMA,
        ],
        compiler_params=pltpu.CompilerParams(
            collective_id=number, has_side_effects=True, vmem_limit_bytes=58 * 2**20
        ),
        cost_estimate=pl.CostEstimate(
            flops=slots * 8 * width**3, bytes_accessed=4 * fields * rows * width * 2, transcendentals=0
        ),
    )(*operands)


def ranked_plan(sink_fields, source_fields, momenta, pair_list, live_pairs):
    devices = lax.axis_size("mom")
    fields, _, rows, width = sink_fields.shape
    slots = pair_list.shape[1]
    places = jnp.arange(devices, dtype=jnp.int32)
    ahead = (live_pairs[None, :] > live_pairs[:, None]) | (
        (live_pairs[None, :] == live_pairs[:, None]) & (places[None, :] < places[:, None])
    )
    ranks = jnp.sum(ahead.astype(jnp.int32), axis=1)
    order = jnp.sum(jnp.where(ranks[None, :] == places[:, None], places[None, :], 0), axis=1)
    over_two = jnp.sum((live_pairs > 2).astype(jnp.int32))
    over_one = jnp.sum((live_pairs > 1).astype(jnp.int32))
    choice = jnp.int32(len(PLANS) - 1)
    for number, (heavy, double) in reversed(list(enumerate(PLANS[:-1]))):
        choice = jnp.where((over_two <= heavy) & (over_one <= heavy + double), number, choice)
    operands = (
        order, ranks, momenta, pair_list, live_pairs,
        sink_fields.reshape(fields, 2 * rows, width), source_fields.reshape(fields, 2 * rows, width),
    )
    branches = [
        functools.partial(
            lambda number, heavy, double, *given: sector_call(
                number, heavy, double, rows, devices, slots, width, given
            ),
            number, heavy, double,
        )
        for number, (heavy, double) in enumerate(PLANS)
    ]
    grams = lax.switch(choice, branches, *operands)
    lower = jnp.transpose(grams.reshape(1, slots, 2, slots), (0, 2, 1, 3))
    diagonal = jnp.eye(slots, dtype=bool)
    return lower + jnp.where(diagonal, 0.0, jnp.swapaxes(lower, 2, 3))


def on_device(sink_fields, source_fields, momenta, pair_list, live_pairs):
    fits = (
        lax.axis_size("mom") == 16
        and pair_list.shape[0] == 16
        and pair_list.shape[1] == 8
        and sink_fields.shape[2] % 8 == 0
        and sink_fields.shape[3] % 128 == 0
        and sink_fields.shape[3] % CHUNK == 0
    )
    plan = ranked_plan if fits else dense_plan
    return plan(sink_fields, source_fields, momenta, pair_list, live_pairs)


def solution(mesh):
    return jax.shard_map(
        on_device,
        mesh=mesh,
        in_specs=(P("groups", None, "mom", None), P("groups", None, "mom", None), P(), P(), P()),
        out_specs=P(("groups", "mom"), None, None, None),
        check_vma=False,
    )
```

```python
import functools

import jax
import jax.numpy as jnp
import numpy as np
from jax import lax
from jax.experimental import pallas as pl
from jax.experimental.pallas import tpu as pltpu
from jax.sharding import PartitionSpec as P


def complex_block(field_pair):
    eigen_width = field_pair.shape[-1]
    left_block = jnp.concatenate([field_pair[0, 0], field_pair[0, 1]], axis=1)
    upper_half = jnp.concatenate([field_pair[1, 0], field_pair[1, 1]], axis=1)
    lower_half = jnp.concatenate([-field_pair[1, 1], field_pair[1, 0]], axis=1)
    right_block = jnp.concatenate([upper_half, lower_half], axis=0)
    joined = jnp.dot(left_block, right_block, preferred_element_type=jnp.float32)
    return jnp.stack([joined[:, :eigen_width], joined[:, eigen_width:]])


def slot_products(blocks):
    item_count = blocks.shape[1]
    eigen_width = blocks.shape[-1]
    storage = jnp.zeros((item_count, 2, eigen_width, eigen_width), jnp.float32)
    slot_blocks = blocks[0]

    def blank_slot(field_pair):
        return jnp.zeros((2, eigen_width, eigen_width), jnp.float32)

    def one_slot(item_index, held_items):
        field_pair = lax.dynamic_index_in_dim(slot_blocks, item_index, 0, keepdims=False)
        result = lax.cond(jnp.any(field_pair != 0), complex_block, blank_slot, field_pair)
        return lax.dynamic_update_index_in_dim(held_items, result, item_index, 0)

    return lax.fori_loop(0, item_count, one_slot, storage)


def contract(left_rows, right_rows):
    return jnp.einsum("spx,sqx->spq", left_rows, right_rows, preferred_element_type=jnp.float32)


def dense_plan(sink_fields, source_fields, momenta, pair_list, live_pairs):
    devices = lax.axis_size("mom")
    position = lax.axis_index("mom")
    sector_count = live_pairs.shape[0]
    owned_count = sector_count // devices
    pair_slots = pair_list.shape[1]
    frames = momenta.shape[0]
    rows_here = sink_fields.shape[2]
    eigen_width = sink_fields.shape[3]
    squares_sink = jnp.sum(jnp.square(sink_fields.astype(jnp.float32)), axis=(1, 2, 3))
    squares_source = jnp.sum(jnp.square(source_fields.astype(jnp.float32)), axis=(1, 2, 3))
    norm_a, norm_b = lax.psum((squares_sink, squares_source), "mom")
    weight_a = 1.0 / jnp.sqrt(norm_a / eigen_width + 1e-06)
    weight_b = 1.0 / jnp.sqrt(norm_b / eigen_width + 1e-06)
    sectors = jnp.arange(sector_count, dtype=jnp.int32)
    labels = jnp.take(pair_list, sectors, axis=0)
    listed = jnp.take(momenta, sectors % frames, axis=0)
    first_field = jnp.take_along_axis(listed, labels[:, :, 0], axis=1)
    second_field = jnp.take_along_axis(listed, labels[:, :, 1], axis=1)
    live_slot = (
        jnp.arange(pair_slots, dtype=jnp.int32)[None, :] < jnp.take(live_pairs, sectors)[:, None]
    )
    live_mask = live_slot.reshape(-1)[:, None, None, None]
    part_sink = jnp.where(live_mask, jnp.take(sink_fields, first_field.reshape(-1), axis=0), 0)
    part_source = jnp.where(live_mask, jnp.take(source_fields, second_field.reshape(-1), axis=0), 0)
    packed = jnp.stack([part_sink, part_source], axis=1).reshape(
        devices, owned_count * pair_slots, 2, 2, rows_here, eigen_width
    )
    products = slot_products(lax.all_to_all(packed, "mom", split_axis=0, concat_axis=4, tiled=True))
    mine_first = lax.dynamic_slice_in_dim(
        first_field, position * owned_count, owned_count, 0
    ).reshape(-1)
    mine_second = lax.dynamic_slice_in_dim(
        second_field, position * owned_count, owned_count, 0
    ).reshape(-1)
    scale_sink = jnp.take(weight_a, mine_first)
    scale_source = jnp.take(weight_b, mine_second)
    shaped = (
        products * scale_sink[:, None, None, None] * scale_source[:, None, None, None]
    ).astype(jnp.bfloat16)
    flattened = shaped.reshape(owned_count, pair_slots, 2, eigen_width * eigen_width)
    turned = jnp.swapaxes(shaped, 2, 3).reshape(
        owned_count, pair_slots, 2, eigen_width * eigen_width
    )
    real_part = contract(flattened[:, :, 0], turned[:, :, 0]) - contract(
        flattened[:, :, 1], turned[:, :, 1]
    )
    imag_part = contract(flattened[:, :, 0], turned[:, :, 1]) + contract(
        flattened[:, :, 1], turned[:, :, 0]
    )
    gram_blocks = jnp.stack([real_part, imag_part], axis=1)
    return gram_blocks


PLANS = (
    (3, 6), (4, 6), (4, 8), (5, 6), (5, 8), (6, 6), (6, 8),
    (7, 5), (7, 7), (8, 4), (8, 8), (9, 4), (10, 6), (16, 0),
)
CHUNK = 64


def place_of_device(device):
    upper, lower, side, core = device // 8, (device // 4) % 2, (device // 2) % 2, device % 2
    return core * 8 + ((upper + lower + 1) % 2) * 4 + ((side + upper) % 2) * 2 + upper


def device_of_place(place):
    core, outer, turn, upper = place // 8, (place // 4) % 2, (place // 2) % 2, place % 2
    return upper * 8 + ((outer + upper + 1) % 2) * 4 + ((turn + upper) % 2) * 2 + core


def rank_of_place(heavy, devices, place):
    if heavy % 2 == 0:
        return place
    light = place - heavy
    moved = heavy + light // 2 + (light % 2) * ((devices + 1 - heavy) // 2)
    return jnp.where(light < 0, place, moved)


def place_of_rank(heavy, devices, rank):
    if heavy % 2 == 0:
        return rank
    light, first = rank - heavy, (devices + 1 - heavy) // 2
    moved = jnp.where(light < first, heavy + 2 * light, heavy + 1 + 2 * (light - first))
    return jnp.where(light < 0, rank, moved)


def sector_kernel(
    heavy, double, rows, order, ranks, momenta, pairs, live, sink_hbm, source_hbm, out_ref,
    sink, source, packed, recv, product, turned, grams,
    load_sem, send_sem, recv_sem, gram_send, gram_recv,
):
    devices, slots, width = grams.shape[0], product.shape[0], sink.shape[2]
    frames = momenta.shape[0]
    field_rows = 2 * rows
    me = lax.axis_index("mom")
    half = devices // 2
    my_half = me // half

    def rank_of_device(device):
        return rank_of_place(heavy, devices, place_of_device(device))

    my_rank = rank_of_device(me)
    is_heavy = (my_rank < heavy).astype(jnp.int32)
    is_double = (my_rank < heavy + double).astype(jnp.int32)

    loads = [
        pltpu.make_async_copy(sink_hbm, sink, load_sem.at[0]),
        pltpu.make_async_copy(source_hbm, source, load_sem.at[1]),
    ]
    for load in loads:
        load.start()
    barrier = pltpu.get_barrier_semaphore()

    @pl.loop(1, devices)
    def _(step):
        pl.semaphore_signal(barrier, inc=1, device_id={"mom": (me + step) % devices})

    pl.semaphore_wait(barrier, devices - 1)
    for load in loads:
        load.wait()

    def fill(target, device, slot):
        sector = order[rank_of_device(device)]
        frame = sector % frames
        target[pl.ds(0, field_rows), :] = sink[momenta[frame, pairs[2 * slot, sector]]]
        target[pl.ds(field_rows, field_rows), :] = source[momenta[frame, pairs[2 * slot + 1, sector]]]

    def send(device, slot):
        fill(packed.at[slot, device], device, slot)
        pltpu.make_async_remote_copy(
            src_ref=packed.at[slot, device],
            dst_ref=recv.at[slot, me],
            send_sem=send_sem.at[slot],
            recv_sem=recv_sem.at[slot],
            device_id={"mom": device},
        ).start()

    for slot in range(2):
        fill(recv.at[slot, me], me, slot)

        @pl.loop(0, devices)
        def _(step):
            device = ((my_half + 1 + step // half) % 2) * half + (me + step) % half
            sends = device != me
            if slot == 1:
                sends = sends & (rank_of_device(device) < heavy + double)

            @pl.when(sends)
            def _():
                send(device, slot)

    @pl.loop(2, slots)
    def _(slot):
        for near in range(2):
            parity = (my_half + 1 + near) % 2
            count = (heavy + 1 - parity) // 2

            @pl.loop(0, count)
            def _(step):
                device = device_of_place(2 * ((me + step) % count) + parity)

                @pl.when(device != me)
                def _():
                    send(device, slot)

                @pl.when(device == me)
                def _():
                    fill(recv.at[slot, me], me, slot)

    product[pl.ds(1, slots - 1)] = jnp.zeros((slots - 1, width, 2 * width), product.dtype)

    used = live[order[my_rank]]

    def parts(slot, start):
        field = recv[slot, :, pl.ds(start, field_rows), :].astype(jnp.float32)
        norm = jnp.sum(jnp.sum(jnp.square(field), axis=(0, 1), keepdims=True)[0], axis=1, keepdims=True)
        weight = 1.0 / jnp.sqrt(norm / width + 1e-06)
        field = field.reshape(devices, 2, rows, width)
        real = field[:, 0].reshape(width, width).astype(jnp.bfloat16)
        imag = field[:, 1].reshape(width, width).astype(jnp.bfloat16)
        return real, imag, weight

    def work(slot, gram):
        arrived = recv.at[slot, pl.ds(0, devices - 1)]
        pltpu.make_async_copy(arrived, arrived, recv_sem.at[slot]).wait()
        a_re, a_im, weight_a = parts(slot, 0)
        b_re, b_im, weight_b = parts(slot, field_rows)
        left = jnp.concatenate([a_re, a_im], axis=1)
        right = jnp.concatenate(
            [jnp.concatenate([b_re, b_im], axis=1), jnp.concatenate([-b_im, b_re], axis=1)], axis=0
        )
        joined = jnp.dot(left, right, preferred_element_type=jnp.float32)
        joined = joined * weight_a * weight_b
        joined = jnp.where(slot < used, joined, 0.0)
        product[slot] = joined.astype(jnp.bfloat16)
        real = joined[:, :width].T.astype(jnp.bfloat16)
        imag = joined[:, width:].T.astype(jnp.bfloat16)
        turned[0] = jnp.concatenate([real, -imag], axis=1)
        turned[1] = jnp.concatenate([imag, real], axis=1)
        sums = jnp.zeros((slots * CHUNK, 2 * CHUNK), jnp.float32)
        for start in range(0, width, CHUNK):
            left_rows = product[:, start : start + CHUNK, :].reshape(slots * CHUNK, 2 * width)
            right_rows = turned[:, start : start + CHUNK, :].reshape(2 * CHUNK, 2 * width)
            sums += lax.dot_general(
                left_rows, right_rows, (((1,), (1,)), ((), ())), preferred_element_type=jnp.float32
            )
        row = lax.broadcasted_iota(jnp.int32, sums.shape, 0) % CHUNK
        column = lax.broadcasted_iota(jnp.int32, sums.shape, 1)
        kept = jnp.where(row == column % CHUNK, sums, 0.0).reshape(slots, CHUNK, 2 * CHUNK)
        kept = jnp.sum(kept, axis=1)
        first_part = lax.broadcasted_iota(jnp.int32, kept.shape, 1) < CHUNK
        real_sum = jnp.sum(jnp.where(first_part, kept, 0.0), axis=1, keepdims=True)
        imag_sum = jnp.sum(jnp.where(first_part, 0.0, kept), axis=1, keepdims=True)
        place = place_in_row - slot
        gram = gram + jnp.where(place == 0, real_sum, 0.0) + jnp.where(place == slots, imag_sum, 0.0)
        return gram

    tile = (slots, 2 * slots * slots)
    place_in_row = lax.broadcasted_iota(jnp.int32, tile, 1) - 2 * slots * lax.broadcasted_iota(jnp.int32, tile, 0)
    gram = lax.fori_loop(0, 1 + is_double + (slots - 2) * is_heavy, work, jnp.zeros(tile, jnp.float32))
    grams[me] = jnp.sum(gram, axis=0, keepdims=True)

    @pl.loop(1, devices)
    def _(step):
        pltpu.make_async_remote_copy(
            src_ref=grams.at[me],
            dst_ref=grams.at[me],
            send_sem=gram_send,
            recv_sem=gram_recv,
            device_id={"mom": (me + step) % devices},
        ).start()

    for semaphore in (gram_send, gram_recv):
        moved = grams.at[pl.ds(0, devices - 1)]
        pltpu.make_async_copy(moved, moved, semaphore).wait()

    for slot in range(slots):
        sent = devices - 1 if slot == 0 else heavy + double - is_double if slot == 1 else heavy - is_heavy

        @pl.loop(0, sent)
        def _(step):
            gone = packed.at[slot, 0]
            pltpu.make_async_copy(gone, gone, send_sem.at[slot]).wait()

    out_ref[...] = grams[device_of_place(place_of_rank(heavy, devices, ranks[me]))]


def sector_call(number, heavy, double, rows, devices, slots, width, operands):
    fields = operands[-1].shape[0]
    piece = 4 * rows
    smem = pl.BlockSpec(memory_space=pltpu.SMEM)
    hbm = pl.BlockSpec(memory_space=pl.ANY)
    low = jnp.bfloat16
    return pl.pallas_call(
        functools.partial(sector_kernel, heavy, double, rows),
        out_shape=jax.ShapeDtypeStruct((1, 2 * slots * slots), jnp.float32),
        in_specs=[smem] * 5 + [hbm] * 2,
        out_specs=pl.BlockSpec(memory_space=pltpu.VMEM),
        scratch_shapes=[
            pltpu.VMEM((fields, 2 * rows, width), low),
            pltpu.VMEM((fields, 2 * rows, width), low),
            pltpu.VMEM((slots, devices, piece, width), low),
            pltpu.VMEM((slots, devices, piece, width), low),
            pltpu.VMEM((slots, width, 2 * width), low),
            pltpu.VMEM((2, width, 2 * width), low),
            pltpu.VMEM((devices, 1, 2 * slots * slots), jnp.float32),
            pltpu.SemaphoreType.DMA((2,)),
            pltpu.SemaphoreType.DMA((slots,)),
            pltpu.SemaphoreType.DMA((slots,)),
            pltpu.SemaphoreType.DMA,
            pltpu.SemaphoreType.DMA,
        ],
        compiler_params=pltpu.CompilerParams(
            collective_id=number, has_side_effects=True, vmem_limit_bytes=58 * 2**20
        ),
        cost_estimate=pl.CostEstimate(
            flops=slots * 8 * width**3, bytes_accessed=4 * fields * rows * width * 2, transcendentals=0
        ),
    )(*operands)


def ranked_plan(sink_fields, source_fields, momenta, pair_list, live_pairs):
    devices = lax.axis_size("mom")
    fields, _, rows, width = sink_fields.shape
    slots = pair_list.shape[1]
    places = jnp.arange(devices, dtype=jnp.int32)
    ahead = (live_pairs[None, :] > live_pairs[:, None]) | (
        (live_pairs[None, :] == live_pairs[:, None]) & (places[None, :] < places[:, None])
    )
    ranks = jnp.sum(ahead.astype(jnp.int32), axis=1)
    order = jnp.sum(jnp.where(ranks[None, :] == places[:, None], places[None, :], 0), axis=1)
    wide = devices + 1
    chosen = np.array(
        [
            next((k for k, (heavy, double) in enumerate(PLANS) if two <= heavy and one <= heavy + double), len(PLANS) - 1)
            for two in range(wide)
            for one in range(wide)
        ],
        np.int32,
    )
    counts = jnp.sum((live_pairs > 2).astype(jnp.int32) * wide + (live_pairs > 1).astype(jnp.int32))
    choice = lax.dynamic_index_in_dim(jnp.asarray(chosen), counts, 0, keepdims=False)
    operands = (
        order, ranks, momenta, jnp.transpose(pair_list, (1, 2, 0)).reshape(2 * slots, devices), live_pairs,
        sink_fields.reshape(fields, 2 * rows, width), source_fields.reshape(fields, 2 * rows, width),
    )
    branches = [
        functools.partial(
            lambda number, heavy, double, *given: sector_call(
                number, heavy, double, rows, devices, slots, width, given
            ),
            number, heavy, double,
        )
        for number, (heavy, double) in enumerate(PLANS)
    ]
    grams = lax.switch(choice, branches, *operands)
    lower = jnp.transpose(grams.reshape(1, slots, 2, slots), (0, 2, 1, 3))
    diagonal = jnp.eye(slots, dtype=bool)
    return lower + jnp.where(diagonal, 0.0, jnp.swapaxes(lower, 2, 3))


def on_device(sink_fields, source_fields, momenta, pair_list, live_pairs):
    fits = (
        lax.axis_size("mom") == 16
        and pair_list.shape[0] == 16
        and pair_list.shape[1] == 8
        and sink_fields.shape[2] % 8 == 0
        and sink_fields.shape[3] % 128 == 0
        and sink_fields.shape[3] % CHUNK == 0
    )
    plan = ranked_plan if fits else dense_plan
    return plan(sink_fields, source_fields, momenta, pair_list, live_pairs)


def solution(mesh):
    return jax.shard_map(
        on_device,
        mesh=mesh,
        in_specs=(P("groups", None, "mom", None), P("groups", None, "mom", None), P(), P(), P()),
        out_specs=P(("groups", "mom"), None, None, None),
        check_vma=False,
    )
```

```python
import functools

import jax
import jax.numpy as jnp
import numpy as np
from jax import lax
from jax.experimental import pallas as pl
from jax.experimental.pallas import tpu as pltpu
from jax.sharding import PartitionSpec as P


def complex_block(field_pair):
    eigen_width = field_pair.shape[-1]
    left_block = jnp.concatenate([field_pair[0, 0], field_pair[0, 1]], axis=1)
    upper_half = jnp.concatenate([field_pair[1, 0], field_pair[1, 1]], axis=1)
    lower_half = jnp.concatenate([-field_pair[1, 1], field_pair[1, 0]], axis=1)
    right_block = jnp.concatenate([upper_half, lower_half], axis=0)
    joined = jnp.dot(left_block, right_block, preferred_element_type=jnp.float32)
    return jnp.stack([joined[:, :eigen_width], joined[:, eigen_width:]])


def slot_products(blocks):
    item_count = blocks.shape[1]
    eigen_width = blocks.shape[-1]
    storage = jnp.zeros((item_count, 2, eigen_width, eigen_width), jnp.float32)
    slot_blocks = blocks[0]

    def blank_slot(field_pair):
        return jnp.zeros((2, eigen_width, eigen_width), jnp.float32)

    def one_slot(item_index, held_items):
        field_pair = lax.dynamic_index_in_dim(slot_blocks, item_index, 0, keepdims=False)
        result = lax.cond(jnp.any(field_pair != 0), complex_block, blank_slot, field_pair)
        return lax.dynamic_update_index_in_dim(held_items, result, item_index, 0)

    return lax.fori_loop(0, item_count, one_slot, storage)


def contract(left_rows, right_rows):
    return jnp.einsum("spx,sqx->spq", left_rows, right_rows, preferred_element_type=jnp.float32)


def dense_plan(sink_fields, source_fields, momenta, pair_list, live_pairs):
    devices = lax.axis_size("mom")
    position = lax.axis_index("mom")
    sector_count = live_pairs.shape[0]
    owned_count = sector_count // devices
    pair_slots = pair_list.shape[1]
    frames = momenta.shape[0]
    rows_here = sink_fields.shape[2]
    eigen_width = sink_fields.shape[3]
    squares_sink = jnp.sum(jnp.square(sink_fields.astype(jnp.float32)), axis=(1, 2, 3))
    squares_source = jnp.sum(jnp.square(source_fields.astype(jnp.float32)), axis=(1, 2, 3))
    norm_a, norm_b = lax.psum((squares_sink, squares_source), "mom")
    weight_a = 1.0 / jnp.sqrt(norm_a / eigen_width + 1e-06)
    weight_b = 1.0 / jnp.sqrt(norm_b / eigen_width + 1e-06)
    sectors = jnp.arange(sector_count, dtype=jnp.int32)
    labels = jnp.take(pair_list, sectors, axis=0)
    listed = jnp.take(momenta, sectors % frames, axis=0)
    first_field = jnp.take_along_axis(listed, labels[:, :, 0], axis=1)
    second_field = jnp.take_along_axis(listed, labels[:, :, 1], axis=1)
    live_slot = (
        jnp.arange(pair_slots, dtype=jnp.int32)[None, :] < jnp.take(live_pairs, sectors)[:, None]
    )
    live_mask = live_slot.reshape(-1)[:, None, None, None]
    part_sink = jnp.where(live_mask, jnp.take(sink_fields, first_field.reshape(-1), axis=0), 0)
    part_source = jnp.where(live_mask, jnp.take(source_fields, second_field.reshape(-1), axis=0), 0)
    packed = jnp.stack([part_sink, part_source], axis=1).reshape(
        devices, owned_count * pair_slots, 2, 2, rows_here, eigen_width
    )
    products = slot_products(lax.all_to_all(packed, "mom", split_axis=0, concat_axis=4, tiled=True))
    mine_first = lax.dynamic_slice_in_dim(
        first_field, position * owned_count, owned_count, 0
    ).reshape(-1)
    mine_second = lax.dynamic_slice_in_dim(
        second_field, position * owned_count, owned_count, 0
    ).reshape(-1)
    scale_sink = jnp.take(weight_a, mine_first)
    scale_source = jnp.take(weight_b, mine_second)
    shaped = (
        products * scale_sink[:, None, None, None] * scale_source[:, None, None, None]
    ).astype(jnp.bfloat16)
    flattened = shaped.reshape(owned_count, pair_slots, 2, eigen_width * eigen_width)
    turned = jnp.swapaxes(shaped, 2, 3).reshape(
        owned_count, pair_slots, 2, eigen_width * eigen_width
    )
    real_part = contract(flattened[:, :, 0], turned[:, :, 0]) - contract(
        flattened[:, :, 1], turned[:, :, 1]
    )
    imag_part = contract(flattened[:, :, 0], turned[:, :, 1]) + contract(
        flattened[:, :, 1], turned[:, :, 0]
    )
    gram_blocks = jnp.stack([real_part, imag_part], axis=1)
    return gram_blocks


PLANS = (
    (3, 6), (4, 6), (4, 8), (5, 6), (5, 8), (6, 6), (6, 8),
    (7, 5), (7, 7), (8, 4), (8, 8), (9, 4), (10, 6), (16, 0),
)
CHUNK = 64


def place_of_device(device):
    upper, lower, side, core = device // 8, (device // 4) % 2, (device // 2) % 2, device % 2
    return core * 8 + ((upper + lower + 1) % 2) * 4 + ((side + upper) % 2) * 2 + upper


def device_of_place(place):
    core, outer, turn, upper = place // 8, (place // 4) % 2, (place // 2) % 2, place % 2
    return upper * 8 + ((outer + upper + 1) % 2) * 4 + ((turn + upper) % 2) * 2 + core


def rank_of_place(heavy, devices, place):
    if heavy % 2 == 0:
        return place
    light = place - heavy
    moved = heavy + light // 2 + (light % 2) * ((devices + 1 - heavy) // 2)
    return jnp.where(light < 0, place, moved)


def place_of_rank(heavy, devices, rank):
    if heavy % 2 == 0:
        return rank
    light, first = rank - heavy, (devices + 1 - heavy) // 2
    moved = jnp.where(light < first, heavy + 2 * light, heavy + 1 + 2 * (light - first))
    return jnp.where(light < 0, rank, moved)


def sector_kernel(
    heavy, double, rows, order, ranks, momenta, pairs, live, sink_hbm, source_hbm, out_ref,
    sink, source, packed, recv, product, turned, grams,
    load_sem, send_sem, recv_sem, gram_send, gram_recv,
):
    devices, slots, width = grams.shape[0], product.shape[0], sink.shape[2]
    frames = momenta.shape[0]
    field_rows = 2 * rows
    me = lax.axis_index("mom")
    half = devices // 2
    my_half = me // half

    def rank_of_device(device):
        return rank_of_place(heavy, devices, place_of_device(device))

    my_rank = rank_of_device(me)
    is_heavy = (my_rank < heavy).astype(jnp.int32)
    is_double = (my_rank < heavy + double).astype(jnp.int32)

    loads = [
        pltpu.make_async_copy(sink_hbm, sink, load_sem.at[0]),
        pltpu.make_async_copy(source_hbm, source, load_sem.at[1]),
    ]
    for load in loads:
        load.start()
    barrier = pltpu.get_barrier_semaphore()

    @pl.loop(1, devices)
    def _(step):
        pl.semaphore_signal(barrier, inc=1, device_id={"mom": (me + step) % devices})

    pl.semaphore_wait(barrier, devices - 1)
    for load in loads:
        load.wait()

    def fill(target, device, slot):
        sector = order[rank_of_device(device)]
        frame = sector % frames
        target[pl.ds(0, field_rows), :] = sink[momenta[frame, pairs[2 * slot, sector]]]
        target[pl.ds(field_rows, field_rows), :] = source[momenta[frame, pairs[2 * slot + 1, sector]]]

    def send(device, slot):
        fill(packed.at[slot, device], device, slot)
        pltpu.make_async_remote_copy(
            src_ref=packed.at[slot, device],
            dst_ref=recv.at[slot, me],
            send_sem=send_sem.at[slot],
            recv_sem=recv_sem.at[slot],
            device_id={"mom": device},
        ).start()

    for slot in range(2):
        fill(recv.at[slot, me], me, slot)

        @pl.loop(0, devices)
        def _(step):
            device = ((my_half + 1 + step // half) % 2) * half + (me + step) % half
            sends = device != me
            if slot == 1:
                sends = sends & (rank_of_device(device) < heavy + double)

            @pl.when(sends)
            def _():
                send(device, slot)

    @pl.loop(2, slots)
    def _(slot):
        for near in range(2):
            parity = (my_half + 1 + near) % 2
            count = (heavy + 1 - parity) // 2

            @pl.loop(0, count)
            def _(step):
                device = device_of_place(2 * ((me + step) % count) + parity)

                @pl.when(device != me)
                def _():
                    send(device, slot)

                @pl.when(device == me)
                def _():
                    fill(recv.at[slot, me], me, slot)

    product[pl.ds(1, slots - 1)] = jnp.zeros((slots - 1, width, 2 * width), product.dtype)

    used = live[order[my_rank]]

    def parts(slot, start):
        field = recv[slot, :, pl.ds(start, field_rows), :].astype(jnp.float32)
        norm = jnp.sum(jnp.sum(jnp.square(field), axis=(0, 1), keepdims=True)[0], axis=1, keepdims=True)
        weight = 1.0 / jnp.sqrt(norm / width + 1e-06)
        field = field.reshape(devices, 2, rows, width)
        real = field[:, 0].reshape(width, width).astype(jnp.bfloat16)
        imag = field[:, 1].reshape(width, width).astype(jnp.bfloat16)
        return real, imag, weight

    def work(slot, gram):
        arrived = recv.at[slot, pl.ds(0, devices - 1)]
        pltpu.make_async_copy(arrived, arrived, recv_sem.at[slot]).wait()
        a_re, a_im, weight_a = parts(slot, 0)
        b_re, b_im, weight_b = parts(slot, field_rows)
        left = jnp.concatenate([a_re, a_im], axis=1)
        right = jnp.concatenate(
            [jnp.concatenate([b_re, b_im], axis=1), jnp.concatenate([-b_im, b_re], axis=1)], axis=0
        )
        joined = jnp.dot(left, right, preferred_element_type=jnp.float32)
        joined = joined * weight_a * weight_b
        joined = jnp.where(slot < used, joined, 0.0)
        product[slot] = joined.astype(jnp.bfloat16)
        real = joined[:, :width].T.astype(jnp.bfloat16)
        imag = joined[:, width:].T.astype(jnp.bfloat16)
        turned[0] = jnp.concatenate([real, -imag], axis=1)
        turned[1] = jnp.concatenate([imag, real], axis=1)
        sums = jnp.zeros((slots * CHUNK, 2 * CHUNK), jnp.float32)
        for start in range(0, width, CHUNK):
            left_rows = product[:, start : start + CHUNK, :].reshape(slots * CHUNK, 2 * width)
            right_rows = turned[:, start : start + CHUNK, :].reshape(2 * CHUNK, 2 * width)
            sums += lax.dot_general(
                left_rows, right_rows, (((1,), (1,)), ((), ())), preferred_element_type=jnp.float32
            )
        row = lax.broadcasted_iota(jnp.int32, sums.shape, 0) % CHUNK
        column = lax.broadcasted_iota(jnp.int32, sums.shape, 1)
        kept = jnp.where(row == column % CHUNK, sums, 0.0).reshape(slots, CHUNK, 2 * CHUNK)
        kept = jnp.sum(kept, axis=1)
        first_part = lax.broadcasted_iota(jnp.int32, kept.shape, 1) < CHUNK
        real_sum = jnp.sum(jnp.where(first_part, kept, 0.0), axis=1, keepdims=True)
        imag_sum = jnp.sum(jnp.where(first_part, 0.0, kept), axis=1, keepdims=True)
        place = place_in_row - slot
        gram = gram + jnp.where(place == 0, real_sum, 0.0) + jnp.where(place == slots, imag_sum, 0.0)
        return gram

    tile = (slots, 2 * slots * slots)
    place_in_row = lax.broadcasted_iota(jnp.int32, tile, 1) - 2 * slots * lax.broadcasted_iota(jnp.int32, tile, 0)
    gram = lax.fori_loop(0, 1 + is_double + (slots - 2) * is_heavy, work, jnp.zeros(tile, jnp.float32))
    grams[me] = jnp.sum(gram, axis=0, keepdims=True)

    @pl.loop(1, devices)
    def _(step):
        pltpu.make_async_remote_copy(
            src_ref=grams.at[me],
            dst_ref=grams.at[me],
            send_sem=gram_send,
            recv_sem=gram_recv,
            device_id={"mom": (me + step) % devices},
        ).start()

    for semaphore in (gram_send, gram_recv):
        moved = grams.at[pl.ds(0, devices - 1)]
        pltpu.make_async_copy(moved, moved, semaphore).wait()

    for slot in range(slots):
        sent = devices - 1 if slot == 0 else heavy + double - is_double if slot == 1 else heavy - is_heavy

        @pl.loop(0, sent)
        def _(step):
            gone = packed.at[slot, 0]
            pltpu.make_async_copy(gone, gone, send_sem.at[slot]).wait()

    out_ref[...] = grams[device_of_place(place_of_rank(heavy, devices, ranks[me]))]


def sector_call(number, heavy, double, rows, devices, slots, width, operands):
    fields = operands[-1].shape[0]
    piece = 4 * rows
    smem = pl.BlockSpec(memory_space=pltpu.SMEM)
    hbm = pl.BlockSpec(memory_space=pl.ANY)
    low = jnp.bfloat16
    return pl.pallas_call(
        functools.partial(sector_kernel, heavy, double, rows),
        out_shape=jax.ShapeDtypeStruct((1, 2 * slots * slots), jnp.float32),
        in_specs=[smem] * 5 + [hbm] * 2,
        out_specs=pl.BlockSpec(memory_space=pltpu.VMEM),
        scratch_shapes=[
            pltpu.VMEM((fields, 2 * rows, width), low),
            pltpu.VMEM((fields, 2 * rows, width), low),
            pltpu.VMEM((slots, devices, piece, width), low),
            pltpu.VMEM((slots, devices, piece, width), low),
            pltpu.VMEM((slots, width, 2 * width), low),
            pltpu.VMEM((2, width, 2 * width), low),
            pltpu.VMEM((devices, 1, 2 * slots * slots), jnp.float32),
            pltpu.SemaphoreType.DMA((2,)),
            pltpu.SemaphoreType.DMA((slots,)),
            pltpu.SemaphoreType.DMA((slots,)),
            pltpu.SemaphoreType.DMA,
            pltpu.SemaphoreType.DMA,
        ],
        compiler_params=pltpu.CompilerParams(
            collective_id=number, has_side_effects=True, vmem_limit_bytes=58 * 2**20
        ),
        cost_estimate=pl.CostEstimate(
            flops=slots * 8 * width**3, bytes_accessed=4 * fields * rows * width * 2, transcendentals=0
        ),
    )(*operands)


def ranked_plan(sink_fields, source_fields, momenta, pair_list, live_pairs):
    devices = lax.axis_size("mom")
    fields, _, rows, width = sink_fields.shape
    slots = pair_list.shape[1]
    places = jnp.arange(devices, dtype=jnp.int32)
    ahead = (live_pairs[None, :] > live_pairs[:, None]) | (
        (live_pairs[None, :] == live_pairs[:, None]) & (places[None, :] < places[:, None])
    )
    ranks = jnp.sum(ahead.astype(jnp.int32), axis=1)
    order = jnp.sum(jnp.where(ranks[None, :] == places[:, None], places[None, :], 0), axis=1)
    wide = devices + 1
    chosen = np.array(
        [
            next((k for k, (heavy, double) in enumerate(PLANS) if two <= heavy and one <= heavy + double), len(PLANS) - 1)
            for two in range(wide)
            for one in range(wide)
        ],
        np.int32,
    )
    counts = jnp.sum((live_pairs > 2).astype(jnp.int32) * wide + (live_pairs > 1).astype(jnp.int32))
    choice = jnp.sum(jnp.where(jnp.arange(wide * wide, dtype=jnp.int32) == counts, jnp.asarray(chosen), 0))
    operands = (
        order, ranks, momenta, jnp.transpose(pair_list, (1, 2, 0)).reshape(2 * slots, devices), live_pairs,
        sink_fields.reshape(fields, 2 * rows, width), source_fields.reshape(fields, 2 * rows, width),
    )
    branches = [
        functools.partial(
            lambda number, heavy, double, *given: sector_call(
                number, heavy, double, rows, devices, slots, width, given
            ),
            number, heavy, double,
        )
        for number, (heavy, double) in enumerate(PLANS)
    ]
    grams = lax.switch(choice, branches, *operands)
    lower = jnp.transpose(grams.reshape(1, slots, 2, slots), (0, 2, 1, 3))
    diagonal = jnp.eye(slots, dtype=bool)
    return lower + jnp.where(diagonal, 0.0, jnp.swapaxes(lower, 2, 3))


def on_device(sink_fields, source_fields, momenta, pair_list, live_pairs):
    fits = (
        lax.axis_size("mom") == 16
        and pair_list.shape[0] == 16
        and pair_list.shape[1] == 8
        and sink_fields.shape[2] % 8 == 0
        and sink_fields.shape[3] % 128 == 0
        and sink_fields.shape[3] % CHUNK == 0
    )
    plan = ranked_plan if fits else dense_plan
    return plan(sink_fields, source_fields, momenta, pair_list, live_pairs)


def solution(mesh):
    return jax.shard_map(
        on_device,
        mesh=mesh,
        in_specs=(P("groups", None, "mom", None), P("groups", None, "mom", None), P(), P(), P()),
        out_specs=P(("groups", "mom"), None, None, None),
        check_vma=False,
    )
```
